32 devices in a mesh: fsdp: 32 (over z, y, x, core).
Axes of the slice: x: 2, y: 2, z: 4, core: 2. Of those that a mesh axis runs over, the one named last changes fastest.
Arguments:
- tokens: bfloat16 [32768, 768], P('fsdp'), may hold values from -6 to 6
- lengths: int32 [64], P('fsdp'), may hold values from 1 to 512, as said below
- query_weight: bfloat16 [768, 768], P('fsdp'), may hold values from -0.4375 to 0.4375
- key_weight: bfloat16 [768, 768], P('fsdp'), may hold values from -0.21875 to 0.21875
- value_weight: bfloat16 [768, 768], P('fsdp'), may hold values from -0.21875 to 0.21875
- out_weight: bfloat16 [768, 768], P('fsdp'), may hold values from -0.875 to 0.875
- query_bias: bfloat16 [768], P('fsdp'), may hold values from -3 to 3
- value_bias: bfloat16 [768], P('fsdp'), may hold values from -3 to 3
- out_bias: bfloat16 [768], P('fsdp'), may hold values from -3 to 3
- first_gain: bfloat16 [768], P('fsdp'), may hold values from 0.099609375 to 1.8984375
- first_shift: bfloat16 [768], P('fsdp'), may hold values from -3 to 3
- up_weight: bfloat16 [768, 3072], P('fsdp'), may hold values from -0.21875 to 0.21875
- down_weight: bfloat16 [3072, 768], P('fsdp'), may hold values from -0.21875 to 0.21875
- up_bias: bfloat16 [3072], P('fsdp'), may hold values from -3 to 3
- down_bias: bfloat16 [768], P('fsdp'), may hold values from -3 to 3
- second_gain: bfloat16 [768], P('fsdp'), may hold values from 0.099609375 to 1.8984375
- second_shift: bfloat16 [768], P('fsdp'), may hold values from -3 to 3
- cotangent: bfloat16 [32768, 768], P('fsdp'), may hold values from -6 to 6
Outputs:
- layer_out: bfloat16 [32768, 768], P('fsdp')
- token_grad: bfloat16 [32768, 768], P('fsdp')
- query_weight_grad: float32 [768, 768], P('fsdp')
- key_weight_grad: float32 [768, 768], P('fsdp')
- value_weight_grad: float32 [768, 768], P('fsdp')
- out_weight_grad: float32 [768, 768], P('fsdp')
- query_bias_grad: float32 [768], P('fsdp')
- value_bias_grad: float32 [768], P('fsdp')
- out_bias_grad: float32 [768], P('fsdp')
- first_gain_grad: float32 [768], P('fsdp')
- first_shift_grad: float32 [768], P('fsdp')
- up_weight_grad: float32 [768, 3072], P('fsdp')
- down_weight_grad: float32 [3072, 768], P('fsdp')
- up_bias_grad: float32 [3072], P('fsdp')
- down_bias_grad: float32 [768], P('fsdp')
- second_gain_grad: float32 [768], P('fsdp')
- second_shift_grad: float32 [768], P('fsdp')
The draws below stay inside these ranges and needn't reach their ends.
Inputs may be any that keep to these rules, and one draw needn't show every extreme that they name: `lengths`: some sequence has exactly 512 valid positions and some exactly 1.
All inputs are finite; a program needn't handle non-finite values.
Results may differ from the reference program's by a relative error of at most 0.015.
The reference program's roundings to bfloat16 on the way count: a program that leaves them out, or rounds other values in their place, can miss the bound.
Values may be sent and summed in bfloat16 or wider, within the bound.
A program may use at most 192 MiB of HBM per device.

```python
import math
import jax
import jax.numpy as jnp
from jax import lax

HEADS = 12
HEAD_DIM = 64
D = 768
FF = 3072
SEQ_LEN = 512
SEQ_DEV = 2
SEQS = 64
TOKENS = 32768


def draw_lengths(key, part):
    key = jax.random.fold_in(key, 11)
    key_base, key_caps, key_first, key_second = jax.random.split(key, 4)
    base = jax.random.randint(key_base, (SEQS // SEQ_DEV, SEQ_DEV), SEQ_LEN // 4, SEQ_LEN + 1)
    caps = jax.random.randint(key_caps, (SEQS // SEQ_DEV, 1), SEQ_LEN // 2, SEQ_LEN + 1)
    result = jnp.minimum(base, caps).reshape(SEQS)
    first = jax.random.randint(key_first, (), 0, SEQS)
    second = (first + 1 + jax.random.randint(key_second, (), 0, SEQS - 1)) % SEQS
    result = result.at[first].set(SEQ_LEN).at[second].set(1)
    return result.astype(jnp.int32)


def spiked(array, own_key, source, target, blocks, factor):
    owner, partner = [(jnp.arange(array.shape[dim]) // (array.shape[dim] // blocks)).reshape([-1 if axis == dim else 1 for axis in range(array.ndim)]) for dim in (source, target)]
    chosen = jax.random.permutation(own_key, blocks)[partner]
    strong = (owner == chosen) | (owner == (partner + blocks // 2) % blocks)
    return jnp.where(strong, factor * array, array)


def block_levels(own_key, extent, cuts, smallest, top_value):
    factor_of, own = 1.0, jax.random.fold_in(own_key, 6)
    for dim, parts in cuts:
        steps = jnp.exp(jax.random.uniform(jax.random.fold_in(own, dim), (parts,), jnp.float32, smallest / len(cuts), top_value / len(cuts)))
        factor_of = factor_of * jnp.repeat(steps, extent[dim] // parts).reshape([-1 if axis == dim else 1 for axis in range(len(extent))])
    return factor_of


def noise(own_key, extent, scale, limit, shards=(), held_as=jnp.bfloat16):
    gain = block_levels(own_key, extent, shards, -0.22, 0.18) if shards else 1.0
    values = jax.random.normal(own_key, extent, jnp.float32) * scale * gain
    return jnp.minimum(jnp.maximum(values, -limit), limit).astype(held_as)


def heavy_noise(own_key, dims, width, limit, pieces, heavy, dtype=jnp.bfloat16):
    drawn = width * jax.random.normal(own_key, dims, jnp.float32)
    if pieces:
        drawn = drawn * block_levels(own_key, dims, pieces, -0.22, 0.18)
    return jnp.clip(spiked(drawn, jax.random.fold_in(own_key, 3), *heavy), -limit, limit).astype(dtype)


def setup_inputs(seed: int = 0) -> dict:
    arg_keys = jax.random.split(jax.random.key(seed), 19)
    tokens = heavy_noise(arg_keys[0], (TOKENS, D), 1.0, 6.0, ((0, 32),), (0, 1, 32, 2.75))
    lengths = draw_lengths(jax.random.fold_in(arg_keys[18], 71), 0)
    query_weight = noise(arg_keys[2], (D, D), (D // 4) ** -0.5, 0.4375, ((0, 32),))
    key_weight = noise(arg_keys[3], (D, D), D ** -0.5, 0.21875, ((0, 32),))
    value_weight = noise(arg_keys[4], (D, D), D ** -0.5, 0.21875, ((0, 32),))
    out_weight = noise(arg_keys[5], (D, D), (D // 16) ** -0.5, 0.875, ((0, 32),))
    query_bias = noise(arg_keys[6], (D,), 0.5, 3.0, ((0, 32),))
    value_bias = noise(arg_keys[7], (D,), 0.5, 3.0, ((0, 32),))
    out_bias = noise(arg_keys[8], (D,), 0.5, 3.0, ((0, 32),))
    first_gain = jnp.clip(1.0 + 0.18 * jax.random.normal(arg_keys[9], (D,), jnp.float32), 0.099609375, 1.8984375).astype(jnp.bfloat16)
    first_shift = noise(arg_keys[10], (D,), 0.5, 3.0, ((0, 32),))
    up_weight = noise(arg_keys[11], (D, FF), D ** -0.5, 0.21875, ((0, 32),))
    down_weight = noise(arg_keys[12], (FF, D), (FF // 4) ** -0.5, 0.21875, ((0, 32),))
    up_bias = noise(arg_keys[13], (FF,), 0.5, 3.0, ((0, 32),))
    down_bias = noise(arg_keys[14], (D,), 0.5, 3.0, ((0, 32),))
    second_gain = jnp.clip(1.0 + 0.18 * jax.random.normal(arg_keys[15], (D,), jnp.float32), 0.099609375, 1.8984375).astype(jnp.bfloat16)
    second_shift = noise(arg_keys[16], (D,), 0.5, 3.0, ((0, 32),))
    cotangent = noise(arg_keys[17], (TOKENS, D), 1.0, 6.0, ((0, 32),))
    return {"tokens": tokens, "lengths": lengths, "query_weight": query_weight, "key_weight": key_weight, "value_weight": value_weight, "out_weight": out_weight, "query_bias": query_bias, "value_bias": value_bias, "out_bias": out_bias, "first_gain": first_gain, "first_shift": first_shift, "up_weight": up_weight, "down_weight": down_weight, "up_bias": up_bias, "down_bias": down_bias, "second_gain": second_gain, "second_shift": second_shift, "cotangent": cotangent}


HIGHEST = lax.Precision.HIGHEST
NEGATIVE = -1e+30
EPSILON = 1e-06

@jax.custom_vjp
def low(v):
    return lax.optimization_barrier(v.astype(jnp.bfloat16)).astype(jnp.float32)

@jax.custom_vjp
def low_back(v):
    return v

def low_keep(v):
    return (low(v), None)

def low_pass(kept, grad):
    return (grad,)

def back_keep(v):
    return (v, None)

def back_low(kept, grad):
    return (low(grad),)
low.defvjp(low_keep, low_pass)
low_back.defvjp(back_keep, back_low)

def layer_norm(hidden, gain_vector, offset):
    center = hidden - lax.optimization_barrier(jnp.mean(hidden, axis=-1, keepdims=True))
    spread = lax.optimization_barrier(jnp.mean(center * center, axis=-1, keepdims=True))
    return center * lax.rsqrt(spread + EPSILON) * gain_vector + offset

def layer_forward(params, tokens_row, length):
    query_weight, key_weight, value_weight, out_weight, query_bias, value_bias, out_bias, first_gain, first_shift, up_weight, down_weight, up_bias, down_bias, second_gain, second_shift = params
    queries = low_back(low(jnp.dot(tokens_row, query_weight, precision=HIGHEST) + query_bias))
    key_vectors = low_back(low(jnp.dot(tokens_row, key_weight, precision=HIGHEST)))
    values = low_back(low(jnp.dot(tokens_row, value_weight, precision=HIGHEST) + value_bias))
    shaped = (SEQ_LEN, HEADS, HEAD_DIM)
    score_scale = 1.0 / math.sqrt(HEAD_DIM)
    scores = low_back(jnp.einsum('qhd,khd->hqk', queries.reshape(shaped), key_vectors.reshape(shaped), precision=HIGHEST) * score_scale)
    key_valid = jnp.arange(SEQ_LEN) < length
    scores = jnp.where(key_valid[None, None, :], scores, NEGATIVE)
    highest_score = lax.optimization_barrier(jnp.max(scores, axis=-1, keepdims=True))
    raised = jnp.exp(scores - highest_score)
    probs = raised / lax.optimization_barrier(jnp.sum(raised, axis=-1, keepdims=True))
    context = jnp.einsum('hqk,khd->qhd', low(probs), values.reshape(shaped), precision=HIGHEST)
    context = low_back(low(context.reshape(SEQ_LEN, HEADS * HEAD_DIM)))
    branch = low_back(jnp.dot(context, out_weight, precision=HIGHEST) + out_bias)
    normed = layer_norm(tokens_row + branch, first_gain, first_shift)
    upward = low_back(jnp.dot(low(normed), up_weight, precision=HIGHEST) + up_bias)
    activated = low(jax.nn.gelu(upward, approximate=False))
    feed = low_back(jnp.dot(activated, down_weight, precision=HIGHEST) + down_bias)
    return layer_norm(normed + feed, second_gain, second_shift)

def reference(tokens, lengths, query_weight, key_weight, value_weight, out_weight, query_bias, value_bias, out_bias, first_gain, first_shift, up_weight, down_weight, up_bias, down_bias, second_gain, second_shift, cotangent):
    params = tuple((weight.astype(jnp.float32) for weight in (query_weight, key_weight, value_weight, out_weight, query_bias, value_bias, out_bias, first_gain, first_shift, up_weight, down_weight, up_bias, down_bias, second_gain, second_shift)))
    model_width = HEADS * HEAD_DIM
    token_rows = tokens.astype(jnp.float32).reshape(SEQS, SEQ_LEN, model_width)
    cotangent_rows = cotangent.astype(jnp.float32).reshape(SEQS, SEQ_LEN, model_width)

    def sequence_step(accumulated, sequence_item):
        tokens_row, cotangent_row, length = sequence_item

        def forward_only(param_tuple, rows_in):
            return layer_forward(param_tuple, rows_in, length)
        output_row, pullback = jax.vjp(forward_only, params, tokens_row)
        row_valid = (jnp.arange(SEQ_LEN) < length).astype(jnp.float32)[:, None]
        param_grads, input_grad = pullback(cotangent_row * row_valid)
        accumulated = tuple((left_side + right_side for left_side, right_side in zip(accumulated, param_grads)))
        return (accumulated, (output_row.astype(jnp.bfloat16), input_grad.astype(jnp.bfloat16)))
    start = tuple((jnp.zeros(weight.shape, jnp.float32) for weight in params))
    gradients, (outputs, input_grads) = lax.scan(sequence_step, start, (token_rows, cotangent_rows, lengths))
    return (outputs.reshape(TOKENS, model_width), input_grads.reshape(TOKENS, model_width), gradients[0], gradients[1], gradients[2], gradients[3], gradients[4], gradients[5], gradients[6], gradients[7], gradients[8], gradients[9], gradients[10], gradients[11], gradients[12], gradients[13], gradients[14])
```

```python
import math

import jax
import jax.numpy as jnp
from jax import lax
from jax.sharding import PartitionSpec as P

HEAD_DIM = 64
NEGATIVE = -1e30
EPSILON = 1e-06


def layer_norm(hidden, gain_vector, offset):
    center = hidden - jnp.mean(hidden, axis=-1, keepdims=True)
    spread = jnp.mean(center * center, axis=-1, keepdims=True)
    return center * lax.rsqrt(spread + EPSILON) * gain_vector + offset


def gelu_exact(upward):
    return jax.nn.gelu(upward, approximate=False)


def times_plain(left_side, right_side):
    return jnp.dot(left_side, right_side, preferred_element_type=jnp.float32)


def times_across(left_side, right_side):
    return lax.dot_general(
        left_side, right_side, (((0,), (0,)), ((), ())), preferred_element_type=jnp.float32
    )


def times_back(left_side, right_side):
    return lax.dot_general(
        left_side, right_side, (((1,), (1,)), ((), ())), preferred_element_type=jnp.float32
    )


def column_sum(matrix):
    return jnp.sum(matrix.astype(jnp.float32), axis=0)


def split_heads(matrix, slot_count):
    row_count, model_width = matrix.shape
    return matrix.reshape(slot_count, row_count // slot_count, model_width // HEAD_DIM, HEAD_DIM)


def merge_heads(tensor):
    return tensor.reshape(tensor.shape[0] * tensor.shape[1], tensor.shape[2] * tensor.shape[3])


def attention_scores(queries, key_vectors, key_valid):
    scores = jnp.einsum("sqhd,skhd->shqk", queries, key_vectors, preferred_element_type=jnp.float32)
    scores = scores * (1.0 / math.sqrt(HEAD_DIM))
    return jnp.where(key_valid[:, None, None, :], scores, NEGATIVE)


def forward_pass(tokens_micro, lengths_micro, attention_full, feed_full):
    (
        query_weight,
        key_weight,
        value_weight,
        out_weight,
        query_bias,
        value_bias,
        out_bias,
        first_gain,
        first_shift,
    ) = attention_full
    up_weight, down_weight, up_bias, down_bias, second_gain, second_shift = feed_full
    slot_count = lengths_micro.shape[0]
    seq_length = tokens_micro.shape[0] // slot_count
    positions = lax.broadcasted_iota(jnp.int32, (slot_count, seq_length), 1)
    key_valid = positions < lengths_micro[:, None]
    queries = (times_plain(tokens_micro, query_weight) + query_bias.astype(jnp.float32)).astype(
        jnp.bfloat16
    )
    key_vectors = times_plain(tokens_micro, key_weight).astype(jnp.bfloat16)
    values = (times_plain(tokens_micro, value_weight) + value_bias.astype(jnp.float32)).astype(
        jnp.bfloat16
    )
    query_heads = split_heads(queries, slot_count)
    value_heads = split_heads(values, slot_count)
    scores = attention_scores(query_heads, split_heads(key_vectors, slot_count), key_valid)
    highest_score = jnp.max(scores, axis=-1, keepdims=True)
    raised = jnp.exp(scores - highest_score)
    totals = jnp.sum(raised, axis=-1, keepdims=True)
    probs = (raised / totals).astype(jnp.bfloat16)
    log_total = highest_score + jnp.log(totals)
    context = jnp.einsum("shqk,skhd->sqhd", probs, value_heads, preferred_element_type=jnp.float32)
    context = merge_heads(context).astype(jnp.bfloat16)
    branch = times_plain(context, out_weight) + out_bias.astype(jnp.float32)
    first_sum = tokens_micro.astype(jnp.float32) + branch
    normed = layer_norm(first_sum, first_gain.astype(jnp.float32), first_shift.astype(jnp.float32))
    normed_low = normed.astype(jnp.bfloat16)
    upward = times_plain(normed_low, up_weight) + up_bias.astype(jnp.float32)
    activated = gelu_exact(upward).astype(jnp.bfloat16)
    second_sum = normed + (times_plain(activated, down_weight) + down_bias.astype(jnp.float32))
    output = layer_norm(
        second_sum, second_gain.astype(jnp.float32), second_shift.astype(jnp.float32)
    )
    stored = (
        tokens_micro,
        key_valid,
        queries,
        key_vectors,
        values,
        log_total,
        context,
        first_sum,
        normed_low,
        upward,
        activated,
        second_sum,
    )
    return (output.astype(jnp.bfloat16), stored)


def backward_pass(stored, cotangent_micro, attention_full, feed_full):
    (
        query_weight,
        key_weight,
        value_weight,
        out_weight,
        query_bias,
        value_bias,
        out_bias,
        first_gain,
        first_shift,
    ) = attention_full
    up_weight, down_weight, up_bias, down_bias, second_gain, second_shift = feed_full
    (
        tokens_micro,
        key_valid,
        queries,
        key_vectors,
        values,
        log_total,
        context,
        first_sum,
        normed_low,
        upward,
        activated,
        second_sum,
    ) = stored
    slot_count = key_valid.shape[0]
    row_valid = key_valid.reshape(-1, 1).astype(jnp.float32)
    grad_output = cotangent_micro.astype(jnp.float32) * row_valid
    _, pull_second = jax.vjp(
        layer_norm, second_sum, second_gain.astype(jnp.float32), second_shift.astype(jnp.float32)
    )
    grad_second, second_gain_term, second_shift_term = pull_second(grad_output)
    grad_feed = grad_second.astype(jnp.bfloat16)
    down_weight_term = times_across(activated, grad_feed)
    down_bias_term = column_sum(grad_feed)
    grad_activated = times_back(grad_feed, down_weight)
    _, pull_gelu = jax.vjp(gelu_exact, upward)
    grad_up = pull_gelu(grad_activated)[0].astype(jnp.bfloat16)
    up_weight_term = times_across(normed_low, grad_up)
    up_bias_term = column_sum(grad_up)
    grad_normed = grad_second + times_back(grad_up, up_weight)
    _, pull_first = jax.vjp(
        layer_norm, first_sum, first_gain.astype(jnp.float32), first_shift.astype(jnp.float32)
    )
    grad_first, first_gain_term, first_shift_term = pull_first(grad_normed)
    grad_branch = grad_first.astype(jnp.bfloat16)
    out_weight_term = times_across(context, grad_branch)
    out_bias_term = column_sum(grad_branch)
    grad_context = split_heads(times_back(grad_branch, out_weight).astype(jnp.bfloat16), slot_count)
    query_heads = split_heads(queries, slot_count)
    key_heads = split_heads(key_vectors, slot_count)
    value_heads = split_heads(values, slot_count)
    probs = jnp.exp(attention_scores(query_heads, key_heads, key_valid) - log_total)
    grad_probs = jnp.einsum(
        "sqhd,skhd->shqk", grad_context, value_heads, preferred_element_type=jnp.float32
    )
    grad_values = jnp.einsum(
        "shqk,sqhd->skhd",
        probs.astype(jnp.bfloat16),
        grad_context,
        preferred_element_type=jnp.float32,
    )
    grad_values = merge_heads(grad_values).astype(jnp.bfloat16)
    row_delta = jnp.sum(grad_probs * probs, axis=-1, keepdims=True)
    grad_scores = (probs * (grad_probs - row_delta)).astype(jnp.bfloat16)
    score_scale = 1.0 / math.sqrt(HEAD_DIM)
    grad_queries = jnp.einsum(
        "shqk,skhd->sqhd", grad_scores, key_heads, preferred_element_type=jnp.float32
    )
    grad_queries = (merge_heads(grad_queries) * score_scale).astype(jnp.bfloat16)
    grad_keys = jnp.einsum(
        "shqk,sqhd->skhd", grad_scores, query_heads, preferred_element_type=jnp.float32
    )
    grad_keys = (merge_heads(grad_keys) * score_scale).astype(jnp.bfloat16)
    query_weight_term = times_across(tokens_micro, grad_queries)
    key_weight_term = times_across(tokens_micro, grad_keys)
    value_weight_term = times_across(tokens_micro, grad_values)
    input_grad = (
        grad_first
        + times_back(grad_queries, query_weight)
        + times_back(grad_keys, key_weight)
        + times_back(grad_values, value_weight)
    ).astype(jnp.bfloat16)
    attention_terms = (
        query_weight_term,
        key_weight_term,
        value_weight_term,
        out_weight_term,
        column_sum(grad_queries),
        column_sum(grad_values),
        out_bias_term,
        first_gain_term,
        first_shift_term,
    )
    feed_terms = (
        up_weight_term,
        down_weight_term,
        up_bias_term,
        down_bias_term,
        second_gain_term,
        second_shift_term,
    )
    return (input_grad, attention_terms, feed_terms)


def pack_rows(pieces, vectors, width, dtype):
    blocks = pieces[0].shape[0]
    line = jnp.concatenate([vector.astype(dtype) for vector in vectors], axis=1)
    used = sum(piece.shape[1] for piece in pieces)
    line_rows = -(-line.shape[1] // width)
    line_rows += -(used + line_rows) % 16
    line = jnp.pad(line, ((0, 0), (0, line_rows * width - line.shape[1])))
    line = line.reshape(blocks, line_rows, width)
    return jnp.concatenate([piece.astype(dtype) for piece in pieces] + [line], axis=1)


def cut_line(line, lengths_of):
    parts = []
    start = 0
    for length in lengths_of:
        parts.append(line[:, start : start + length])
        start += length
    return parts


def shards(
    tokens,
    lengths,
    query_weight,
    key_weight,
    value_weight,
    out_weight,
    query_bias,
    value_bias,
    out_bias,
    first_gain,
    first_shift,
    up_weight,
    down_weight,
    up_bias,
    down_bias,
    second_gain,
    second_shift,
    cotangent,
):
    own_rows, width = query_weight.shape
    feed_rows = down_weight.shape[0]
    fold = up_weight.shape[1] // width
    device_count = width // own_rows
    feed_width = feed_rows * device_count

    def up_pieces(matrix, blocks):
        return [
            matrix[:, part * width : (part + 1) * width].reshape(blocks, -1, width)
            for part in range(fold)
        ]

    vectors = (
        query_bias,
        value_bias,
        out_bias,
        first_gain,
        first_shift,
        down_bias,
        second_gain,
        second_shift,
        up_bias,
    )
    packed = pack_rows(
        [query_weight[None], key_weight[None], value_weight[None], out_weight[None]]
        + up_pieces(up_weight, 1)
        + [down_weight[None]],
        [vector[None] for vector in vectors],
        width,
        jnp.bfloat16,
    )
    gathered = lax.all_gather(packed[0], "fsdp", axis=0, tiled=False)
    square = [
        gathered[:, part * own_rows : (part + 1) * own_rows].reshape(width, width)
        for part in range(4 + fold)
    ]
    down_start = (4 + fold) * own_rows
    down_full = gathered[:, down_start : down_start + feed_rows].reshape(feed_width, width)
    line = gathered[:, down_start + feed_rows :].reshape(device_count, -1)
    lines = cut_line(line, [vector.shape[0] for vector in vectors])
    lines = [part.reshape(-1) for part in lines]
    attention_full = tuple(square[:4]) + tuple(lines[:5])
    feed_full = (
        jnp.concatenate(square[4:], axis=1),
        down_full,
        lines[8],
        lines[5],
        lines[6],
        lines[7],
    )

    output, stored = forward_pass(tokens, lengths, attention_full, feed_full)
    input_grad, attention_terms, feed_terms = backward_pass(
        stored, cotangent, attention_full, feed_full
    )

    def to_blocks(matrix):
        return matrix.reshape(device_count, -1, width)

    def to_lines(vector):
        return vector.reshape(device_count, -1)

    up_term, down_term, up_bias_term, down_bias_term, gain_term, shift_term = feed_terms
    feed_packed = pack_rows(
        up_pieces(up_term, device_count) + [to_blocks(down_term)],
        [to_lines(part) for part in (up_bias_term, down_bias_term, gain_term, shift_term)],
        width,
        jnp.bfloat16,
    )
    feed_owned = lax.psum_scatter(
        feed_packed.reshape(-1, width), "fsdp", scatter_dimension=0, tiled=True
    )
    attention_packed = pack_rows(
        [to_blocks(part) for part in attention_terms[:4]],
        [to_lines(part) for part in attention_terms[4:]],
        width,
        jnp.bfloat16,
    )
    attention_owned = lax.psum_scatter(
        attention_packed.reshape(-1, width), "fsdp", scatter_dimension=0, tiled=True
    )
    feed_owned = feed_owned.astype(jnp.float32)
    attention_owned = attention_owned.astype(jnp.float32)
    up_owned = jnp.concatenate(
        [feed_owned[part * own_rows : (part + 1) * own_rows] for part in range(fold)], axis=1
    )
    down_owned = feed_owned[fold * own_rows : fold * own_rows + feed_rows]
    feed_line = feed_owned[fold * own_rows + feed_rows :].reshape(1, -1)
    feed_vectors = [
        part[0] for part in cut_line(feed_line, [feed_rows, own_rows, own_rows, own_rows])
    ]
    squares_owned = [
        attention_owned[part * own_rows : (part + 1) * own_rows] for part in range(4)
    ]
    attention_line = attention_owned[4 * own_rows :].reshape(1, -1)
    attention_vectors = [part[0] for part in cut_line(attention_line, [own_rows] * 5)]
    return (
        output,
        input_grad,
        *squares_owned,
        *attention_vectors,
        up_owned,
        down_owned,
        *feed_vectors,
    )


def solution(mesh):
    return jax.shard_map(
        shards,
        mesh=mesh,
        in_specs=(
            P("fsdp", None),
            P("fsdp"),
            P("fsdp", None),
            P("fsdp", None),
            P("fsdp", None),
            P("fsdp", None),
            P("fsdp"),
            P("fsdp"),
            P("fsdp"),
            P("fsdp"),
            P("fsdp"),
            P("fsdp", None),
            P("fsdp", None),
            P("fsdp"),
            P("fsdp"),
            P("fsdp"),
            P("fsdp"),
            P("fsdp", None),
        ),
        out_specs=(
            P("fsdp", None),
            P("fsdp", None),
            P("fsdp", None),
            P("fsdp", None),
            P("fsdp", None),
            P("fsdp", None),
            P("fsdp"),
            P("fsdp"),
            P("fsdp"),
            P("fsdp"),
            P("fsdp"),
            P("fsdp", None),
            P("fsdp", None),
            P("fsdp"),
            P("fsdp"),
            P("fsdp"),
            P("fsdp"),
        ),
        check_vma=False,
    )
```

```python
import math

import jax
import jax.numpy as jnp
from jax import lax
from jax.sharding import PartitionSpec as P

HEAD_DIM = 64
NEGATIVE = -1e30
EPSILON = 1e-06


def layer_norm(hidden, gain_vector, offset):
    center = hidden - jnp.mean(hidden, axis=-1, keepdims=True)
    spread = jnp.mean(center * center, axis=-1, keepdims=True)
    return center * lax.rsqrt(spread + EPSILON) * gain_vector + offset


def gelu_exact(upward):
    return upward * (0.5 + 0.5 * lax.erf(upward * math.sqrt(0.5)))


def times_plain(left_side, right_side):
    return jnp.dot(left_side, right_side, preferred_element_type=jnp.float32)


def times_across(left_side, right_side):
    return lax.dot_general(
        left_side, right_side, (((0,), (0,)), ((), ())), preferred_element_type=jnp.float32
    )


def times_back(left_side, right_side):
    return lax.dot_general(
        left_side, right_side, (((1,), (1,)), ((), ())), preferred_element_type=jnp.float32
    )


def column_sum(matrix):
    return jnp.sum(matrix.astype(jnp.float32), axis=0)


def split_heads(matrix, slot_count):
    row_count, model_width = matrix.shape
    return matrix.reshape(slot_count, row_count // slot_count, model_width // HEAD_DIM, HEAD_DIM)


def merge_heads(tensor):
    return tensor.reshape(tensor.shape[0] * tensor.shape[1], tensor.shape[2] * tensor.shape[3])


def attention_scores(queries, key_vectors, key_valid):
    scores = jnp.einsum("sqhd,skhd->shqk", queries, key_vectors, preferred_element_type=jnp.float32)
    scores = scores * (1.0 / math.sqrt(HEAD_DIM))
    return jnp.where(key_valid[:, None, None, :], scores, NEGATIVE)


def forward_pass(tokens_micro, lengths_micro, attention_full, feed_full):
    (
        query_weight,
        key_weight,
        value_weight,
        out_weight,
        query_bias,
        value_bias,
        out_bias,
        first_gain,
        first_shift,
    ) = attention_full
    up_weight, down_weight, up_bias, down_bias, second_gain, second_shift = feed_full
    slot_count = lengths_micro.shape[0]
    seq_length = tokens_micro.shape[0] // slot_count
    positions = lax.broadcasted_iota(jnp.int32, (slot_count, seq_length), 1)
    key_valid = positions < lengths_micro[:, None]
    queries = (times_plain(tokens_micro, query_weight) + query_bias.astype(jnp.float32)).astype(
        jnp.bfloat16
    )
    key_vectors = times_plain(tokens_micro, key_weight).astype(jnp.bfloat16)
    values = (times_plain(tokens_micro, value_weight) + value_bias.astype(jnp.float32)).astype(
        jnp.bfloat16
    )
    query_heads = split_heads(queries, slot_count)
    value_heads = split_heads(values, slot_count)
    scores = attention_scores(query_heads, split_heads(key_vectors, slot_count), key_valid)
    highest_score = jnp.max(scores, axis=-1, keepdims=True)
    raised = jnp.exp(scores - highest_score)
    totals = jnp.sum(raised, axis=-1, keepdims=True)
    probs = (raised / totals).astype(jnp.bfloat16)
    log_total = highest_score + jnp.log(totals)
    context = jnp.einsum("shqk,skhd->sqhd", probs, value_heads, preferred_element_type=jnp.float32)
    context = merge_heads(context).astype(jnp.bfloat16)
    branch = times_plain(context, out_weight) + out_bias.astype(jnp.float32)
    first_sum = tokens_micro.astype(jnp.float32) + branch
    normed = layer_norm(first_sum, first_gain.astype(jnp.float32), first_shift.astype(jnp.float32))
    normed_low = normed.astype(jnp.bfloat16)
    upward = times_plain(normed_low, up_weight) + up_bias.astype(jnp.float32)
    activated = gelu_exact(upward).astype(jnp.bfloat16)
    second_sum = normed + (times_plain(activated, down_weight) + down_bias.astype(jnp.float32))
    output = layer_norm(
        second_sum, second_gain.astype(jnp.float32), second_shift.astype(jnp.float32)
    )
    stored = (
        tokens_micro,
        key_valid,
        queries,
        key_vectors,
        values,
        log_total,
        context,
        first_sum,
        normed_low,
        upward,
        activated,
        second_sum,
    )
    return (output.astype(jnp.bfloat16), stored)


def backward_pass(stored, cotangent_micro, attention_full, feed_full):
    (
        query_weight,
        key_weight,
        value_weight,
        out_weight,
        query_bias,
        value_bias,
        out_bias,
        first_gain,
        first_shift,
    ) = attention_full
    up_weight, down_weight, up_bias, down_bias, second_gain, second_shift = feed_full
    (
        tokens_micro,
        key_valid,
        queries,
        key_vectors,
        values,
        log_total,
        context,
        first_sum,
        normed_low,
        upward,
        activated,
        second_sum,
    ) = stored
    slot_count = key_valid.shape[0]
    row_valid = key_valid.reshape(-1, 1).astype(jnp.float32)
    grad_output = cotangent_micro.astype(jnp.float32) * row_valid
    _, pull_second = jax.vjp(
        layer_norm, second_sum, second_gain.astype(jnp.float32), second_shift.astype(jnp.float32)
    )
    grad_second, second_gain_term, second_shift_term = pull_second(grad_output)
    grad_feed = grad_second.astype(jnp.bfloat16)
    down_weight_term = times_across(activated, grad_feed)
    down_bias_term = column_sum(grad_feed)
    grad_activated = times_back(grad_feed, down_weight)
    _, pull_gelu = jax.vjp(gelu_exact, upward)
    grad_up = pull_gelu(grad_activated)[0].astype(jnp.bfloat16)
    up_weight_term = times_across(normed_low, grad_up)
    up_bias_term = column_sum(grad_up)
    grad_normed = grad_second + times_back(grad_up, up_weight)
    _, pull_first = jax.vjp(
        layer_norm, first_sum, first_gain.astype(jnp.float32), first_shift.astype(jnp.float32)
    )
    grad_first, first_gain_term, first_shift_term = pull_first(grad_normed)
    grad_branch = grad_first.astype(jnp.bfloat16)
    out_weight_term = times_across(context, grad_branch)
    out_bias_term = column_sum(grad_branch)
    grad_context = split_heads(times_back(grad_branch, out_weight).astype(jnp.bfloat16), slot_count)
    query_heads = split_heads(queries, slot_count)
    key_heads = split_heads(key_vectors, slot_count)
    value_heads = split_heads(values, slot_count)
    probs = jnp.exp(attention_scores(query_heads, key_heads, key_valid) - log_total)
    grad_probs = jnp.einsum(
        "sqhd,skhd->shqk", grad_context, value_heads, preferred_element_type=jnp.float32
    )
    grad_values = jnp.einsum(
        "shqk,sqhd->skhd",
        probs.astype(jnp.bfloat16),
        grad_context,
        preferred_element_type=jnp.float32,
    )
    grad_values = merge_heads(grad_values).astype(jnp.bfloat16)
    row_delta = jnp.sum(grad_probs * probs, axis=-1, keepdims=True)
    grad_scores = (probs * (grad_probs - row_delta)).astype(jnp.bfloat16)
    score_scale = 1.0 / math.sqrt(HEAD_DIM)
    grad_queries = jnp.einsum(
        "shqk,skhd->sqhd", grad_scores, key_heads, preferred_element_type=jnp.float32
    )
    grad_queries = (merge_heads(grad_queries) * score_scale).astype(jnp.bfloat16)
    grad_keys = jnp.einsum(
        "shqk,sqhd->skhd", grad_scores, query_heads, preferred_element_type=jnp.float32
    )
    grad_keys = (merge_heads(grad_keys) * score_scale).astype(jnp.bfloat16)
    query_weight_term = times_across(tokens_micro, grad_queries)
    key_weight_term = times_across(tokens_micro, grad_keys)
    value_weight_term = times_across(tokens_micro, grad_values)
    input_grad = (
        grad_first
        + times_back(grad_queries, query_weight)
        + times_back(grad_keys, key_weight)
        + times_back(grad_values, value_weight)
    ).astype(jnp.bfloat16)
    attention_terms = (
        query_weight_term,
        key_weight_term,
        value_weight_term,
        out_weight_term,
        column_sum(grad_queries),
        column_sum(grad_values),
        out_bias_term,
        first_gain_term,
        first_shift_term,
    )
    feed_terms = (
        up_weight_term,
        down_weight_term,
        up_bias_term,
        down_bias_term,
        second_gain_term,
        second_shift_term,
    )
    return (input_grad, attention_terms, feed_terms)


def axis_sizes(device_count):
    side = 1
    while 2 * (2 * side) ** 3 <= device_count:
        side *= 2
    return (device_count // (2 * side * side), side, side, 2)


def axis_digit(sizes, axis):
    stride = math.prod(sizes[axis + 1 :])
    return stride, (lax.axis_index("fsdp") // stride) % sizes[axis]


def shifted_pairs(sizes, axis, shift):
    stride = math.prod(sizes[axis + 1 :])
    pairs = []
    for index in range(math.prod(sizes)):
        digit = (index // stride) % sizes[axis]
        pairs.append((index, index + ((digit + shift) % sizes[axis] - digit) * stride))
    return pairs


def scatter_sum(blocks, sizes, order):
    remaining = [0, 1, 2, 3]
    held = blocks.reshape(sizes + blocks.shape[1:])
    for axis in order:
        place = remaining.index(axis)
        _, digit = axis_digit(sizes, axis)
        held = held.astype(jnp.bfloat16)
        arrived = []
        for shift in range(1, sizes[axis]):
            target = (digit + shift) % sizes[axis]
            part = lax.dynamic_index_in_dim(held, target, place, keepdims=False)
            arrived.append(lax.ppermute(part, "fsdp", shifted_pairs(sizes, axis, shift)))
        own = lax.dynamic_index_in_dim(held, digit, place, keepdims=False)
        held = own.astype(jnp.float32)
        for part in arrived:
            held = held + part.astype(jnp.float32)
        remaining.remove(axis)
    return held


def gather_blocks(own, sizes, order):
    present = []
    held = own
    for axis in order:
        place = sum(1 for other in present if other < axis)
        _, digit = axis_digit(sizes, axis)
        shape = held.shape[:place] + (sizes[axis],) + held.shape[place:]
        joined = lax.dynamic_update_index_in_dim(
            jnp.zeros(shape, held.dtype), held, digit, place
        )
        for shift in range(1, sizes[axis]):
            part = lax.ppermute(held, "fsdp", shifted_pairs(sizes, axis, shift))
            source = (digit - shift) % sizes[axis]
            joined = lax.dynamic_update_index_in_dim(joined, part, source, place)
        held = joined
        present.append(axis)
    return held.reshape((math.prod(sizes),) + own.shape)


X_FIRST = (3, 2, 1, 0)
Y_FIRST = (3, 1, 2, 0)


def pack_rows(pieces, vectors, width, dtype):
    blocks = pieces[0].shape[0]
    line = jnp.concatenate([vector.astype(dtype) for vector in vectors], axis=1)
    used = sum(piece.shape[1] for piece in pieces)
    line_rows = -(-line.shape[1] // width)
    line_rows += -(used + line_rows) % 16
    line = jnp.pad(line, ((0, 0), (0, line_rows * width - line.shape[1])))
    line = line.reshape(blocks, line_rows, width)
    return jnp.concatenate([piece.astype(dtype) for piece in pieces] + [line], axis=1)


def cut_line(line, lengths_of):
    parts = []
    start = 0
    for length in lengths_of:
        parts.append(line[:, start : start + length])
        start += length
    return parts


def shards(
    tokens,
    lengths,
    query_weight,
    key_weight,
    value_weight,
    out_weight,
    query_bias,
    value_bias,
    out_bias,
    first_gain,
    first_shift,
    up_weight,
    down_weight,
    up_bias,
    down_bias,
    second_gain,
    second_shift,
    cotangent,
):
    own_rows, width = query_weight.shape
    feed_rows = down_weight.shape[0]
    fold = up_weight.shape[1] // width
    device_count = width // own_rows
    feed_width = feed_rows * device_count

    def up_pieces(matrix, blocks):
        return [
            matrix[:, part * width : (part + 1) * width].reshape(blocks, -1, width)
            for part in range(fold)
        ]

    sizes = axis_sizes(device_count)

    feed_vectors = (up_bias, down_bias, second_gain, second_shift)
    feed_packed = pack_rows(
        up_pieces(up_weight, 1) + [down_weight[None]],
        [vector[None] for vector in feed_vectors],
        width,
        jnp.bfloat16,
    )
    gathered = lax.all_gather(feed_packed[0], "fsdp", axis=0, tiled=False)
    up_full = jnp.concatenate(
        [
            gathered[:, part * own_rows : (part + 1) * own_rows].reshape(width, width)
            for part in range(fold)
        ],
        axis=1,
    )
    down_start = fold * own_rows
    down_full = gathered[:, down_start : down_start + feed_rows].reshape(feed_width, width)
    line = gathered[:, down_start + feed_rows :].reshape(device_count, -1)
    lines = cut_line(line, [vector.shape[0] for vector in feed_vectors])
    feed_full = (up_full, down_full) + tuple(part.reshape(-1) for part in lines)

    vectors = (query_bias, value_bias, out_bias, first_gain, first_shift)
    near = pack_rows(
        [query_weight[None], key_weight[None]],
        [vector[None] for vector in vectors],
        width,
        jnp.bfloat16,
    )
    near = gather_blocks(near[0], sizes, X_FIRST[::-1])
    far = gather_blocks(
        jnp.concatenate([value_weight, out_weight], axis=0), sizes, Y_FIRST[::-1]
    )
    square = [
        array[:, part * own_rows : (part + 1) * own_rows].reshape(width, width)
        for array in (near, far)
        for part in range(2)
    ]
    line = near[:, 2 * own_rows :].reshape(device_count, -1)
    lines = cut_line(line, [own_rows] * 5)
    attention_full = tuple(square) + tuple(part.reshape(-1) for part in lines)

    output, stored = forward_pass(tokens, lengths, attention_full, feed_full)
    input_grad, attention_terms, feed_terms = backward_pass(
        stored, cotangent, attention_full, feed_full
    )

    def to_blocks(matrix):
        return matrix.reshape(device_count, -1, width)

    def to_lines(vector):
        return vector.reshape(device_count, -1)

    up_term, down_term, up_bias_term, down_bias_term, gain_term, shift_term = feed_terms
    down_packed = pack_rows(
        [to_blocks(down_term)],
        [to_lines(part) for part in (up_bias_term, down_bias_term, gain_term, shift_term)],
        width,
        jnp.bfloat16,
    )
    down_sum = scatter_sum(down_packed, sizes, X_FIRST)
    up_sum = scatter_sum(
        jnp.concatenate(
            [part.astype(jnp.bfloat16) for part in up_pieces(up_term, device_count)], axis=1
        ),
        sizes,
        Y_FIRST,
    )
    query_term, key_term, value_term, out_term = [to_blocks(part) for part in attention_terms[:4]]
    far_sum = scatter_sum(
        jnp.concatenate([value_term, out_term], axis=1).astype(jnp.bfloat16), sizes, X_FIRST
    )
    near_sum = scatter_sum(
        pack_rows(
            [query_term, key_term],
            [to_lines(part) for part in attention_terms[4:]],
            width,
            jnp.bfloat16,
        ),
        sizes,
        Y_FIRST,
    )
    up_owned = jnp.concatenate(
        [up_sum[part * own_rows : (part + 1) * own_rows] for part in range(fold)], axis=1
    )
    down_owned = down_sum[:feed_rows]
    feed_line = down_sum[feed_rows:].reshape(1, -1)
    feed_vectors = [
        part[0] for part in cut_line(feed_line, [feed_rows, own_rows, own_rows, own_rows])
    ]
    squares_owned = [
        array[part * own_rows : (part + 1) * own_rows]
        for array in (near_sum, far_sum)
        for part in range(2)
    ]
    attention_line = near_sum[2 * own_rows :].reshape(1, -1)
    attention_vectors = [part[0] for part in cut_line(attention_line, [own_rows] * 5)]
    return (
        output,
        input_grad,
        *squares_owned,
        *attention_vectors,
        up_owned,
        down_owned,
        *feed_vectors,
    )


def solution(mesh):
    return jax.shard_map(
        shards,
        mesh=mesh,
        in_specs=(
            P("fsdp", None),
            P("fsdp"),
            P("fsdp", None),
            P("fsdp", None),
            P("fsdp", None),
            P("fsdp", None),
            P("fsdp"),
            P("fsdp"),
            P("fsdp"),
            P("fsdp"),
            P("fsdp"),
            P("fsdp", None),
            P("fsdp", None),
            P("fsdp"),
            P("fsdp"),
            P("fsdp"),
            P("fsdp"),
            P("fsdp", None),
        ),
        out_specs=(
            P("fsdp", None),
            P("fsdp", None),
            P("fsdp", None),
            P("fsdp", None),
            P("fsdp", None),
            P("fsdp", None),
            P("fsdp"),
            P("fsdp"),
            P("fsdp"),
            P("fsdp"),
            P("fsdp"),
            P("fsdp", None),
            P("fsdp", None),
            P("fsdp"),
            P("fsdp"),
            P("fsdp"),
            P("fsdp"),
        ),
        check_vma=False,
    )
```

```python
import math

import jax
import jax.numpy as jnp
from jax import lax
from jax.sharding import PartitionSpec as P

HEAD_DIM = 64
NEGATIVE = -1e30
EPSILON = 1e-06


def layer_norm(hidden, gain_vector, offset):
    center = hidden - jnp.mean(hidden, axis=-1, keepdims=True)
    spread = jnp.mean(center * center, axis=-1, keepdims=True)
    return center * lax.rsqrt(spread + EPSILON) * gain_vector + offset


def gelu_exact(upward):
    return upward * (0.5 + 0.5 * lax.erf(upward * math.sqrt(0.5)))


def times_plain(left_side, right_side):
    return jnp.dot(left_side, right_side, preferred_element_type=jnp.float32)


def times_across(left_side, right_side):
    return lax.dot_general(
        left_side, right_side, (((0,), (0,)), ((), ())), preferred_element_type=jnp.float32
    )


def times_back(left_side, right_side):
    return lax.dot_general(
        left_side, right_side, (((1,), (1,)), ((), ())), preferred_element_type=jnp.float32
    )


def column_sum(matrix):
    return jnp.sum(matrix.astype(jnp.float32), axis=0)


def split_heads(matrix, slot_count):
    row_count, model_width = matrix.shape
    return matrix.reshape(slot_count, row_count // slot_count, model_width // HEAD_DIM, HEAD_DIM)


def merge_heads(tensor):
    return tensor.reshape(tensor.shape[0] * tensor.shape[1], tensor.shape[2] * tensor.shape[3])


def attention_scores(queries, key_vectors, key_valid):
    scores = jnp.einsum("sqhd,skhd->shqk", queries, key_vectors, preferred_element_type=jnp.float32)
    scores = scores * (1.0 / math.sqrt(HEAD_DIM))
    return jnp.where(key_valid[:, None, None, :], scores, NEGATIVE)


def forward_pass(tokens_micro, lengths_micro, attention_full, feed_full):
    (
        query_weight,
        key_weight,
        value_weight,
        out_weight,
        query_bias,
        value_bias,
        out_bias,
        first_gain,
        first_shift,
    ) = attention_full
    up_weight, down_weight, up_bias, down_bias, second_gain, second_shift = feed_full
    slot_count = lengths_micro.shape[0]
    seq_length = tokens_micro.shape[0] // slot_count
    positions = lax.broadcasted_iota(jnp.int32, (slot_count, seq_length), 1)
    key_valid = positions < lengths_micro[:, None]
    queries = (times_plain(tokens_micro, query_weight) + query_bias.astype(jnp.float32)).astype(
        jnp.bfloat16
    )
    key_vectors = times_plain(tokens_micro, key_weight).astype(jnp.bfloat16)
    values = (times_plain(tokens_micro, value_weight) + value_bias.astype(jnp.float32)).astype(
        jnp.bfloat16
    )
    query_heads = split_heads(queries, slot_count)
    value_heads = split_heads(values, slot_count)
    scores = attention_scores(query_heads, split_heads(key_vectors, slot_count), key_valid)
    highest_score = jnp.max(scores, axis=-1, keepdims=True)
    raised = jnp.exp(scores - highest_score)
    totals = jnp.sum(raised, axis=-1, keepdims=True)
    probs = (raised / totals).astype(jnp.bfloat16)
    log_total = highest_score + jnp.log(totals)
    context = jnp.einsum("shqk,skhd->sqhd", probs, value_heads, preferred_element_type=jnp.float32)
    context = merge_heads(context).astype(jnp.bfloat16)
    branch = times_plain(context, out_weight) + out_bias.astype(jnp.float32)
    first_sum = tokens_micro.astype(jnp.float32) + branch
    normed = layer_norm(first_sum, first_gain.astype(jnp.float32), first_shift.astype(jnp.float32))
    normed_low = normed.astype(jnp.bfloat16)
    upward = times_plain(normed_low, up_weight) + up_bias.astype(jnp.float32)
    activated = gelu_exact(upward).astype(jnp.bfloat16)
    second_sum = normed + (times_plain(activated, down_weight) + down_bias.astype(jnp.float32))
    output = layer_norm(
        second_sum, second_gain.astype(jnp.float32), second_shift.astype(jnp.float32)
    )
    stored = (
        tokens_micro,
        key_valid,
        queries,
        key_vectors,
        values,
        log_total,
        context,
        first_sum,
        normed_low,
        upward,
        activated,
        second_sum,
    )
    return (output.astype(jnp.bfloat16), stored)


def backward_pass(stored, cotangent_micro, attention_full, feed_full, feed_reduce):
    (
        query_weight,
        key_weight,
        value_weight,
        out_weight,
        query_bias,
        value_bias,
        out_bias,
        first_gain,
        first_shift,
    ) = attention_full
    up_weight, down_weight, up_bias, down_bias, second_gain, second_shift = feed_full
    (
        tokens_micro,
        key_valid,
        queries,
        key_vectors,
        values,
        log_total,
        context,
        first_sum,
        normed_low,
        upward,
        activated,
        second_sum,
    ) = stored
    slot_count = key_valid.shape[0]
    row_valid = key_valid.reshape(-1, 1).astype(jnp.float32)
    grad_output = cotangent_micro.astype(jnp.float32) * row_valid
    _, pull_second = jax.vjp(
        layer_norm, second_sum, second_gain.astype(jnp.float32), second_shift.astype(jnp.float32)
    )
    grad_second, second_gain_term, second_shift_term = pull_second(grad_output)
    grad_feed = grad_second.astype(jnp.bfloat16)
    down_weight_term = times_across(activated, grad_feed)
    down_bias_term = column_sum(grad_feed)
    grad_activated = times_back(grad_feed, down_weight)
    _, pull_gelu = jax.vjp(gelu_exact, upward)
    grad_up = pull_gelu(grad_activated)[0].astype(jnp.bfloat16)
    up_weight_term = times_across(normed_low, grad_up)
    up_bias_term = column_sum(grad_up)
    grad_normed = grad_second + times_back(grad_up, up_weight)
    _, pull_first = jax.vjp(
        layer_norm, first_sum, first_gain.astype(jnp.float32), first_shift.astype(jnp.float32)
    )
    grad_first, first_gain_term, first_shift_term = pull_first(grad_normed)
    grad_branch = grad_first.astype(jnp.bfloat16)
    out_weight_term = times_across(context, grad_branch)
    out_bias_term = column_sum(grad_branch)
    grad_context = split_heads(times_back(grad_branch, out_weight).astype(jnp.bfloat16), slot_count)
    query_heads = split_heads(queries, slot_count)
    key_heads = split_heads(key_vectors, slot_count)
    value_heads = split_heads(values, slot_count)
    probs = jnp.exp(attention_scores(query_heads, key_heads, key_valid) - log_total)
    grad_probs = jnp.einsum(
        "sqhd,skhd->shqk", grad_context, value_heads, preferred_element_type=jnp.float32
    )
    grad_values = jnp.einsum(
        "shqk,sqhd->skhd",
        probs.astype(jnp.bfloat16),
        grad_context,
        preferred_element_type=jnp.float32,
    )
    grad_values = merge_heads(grad_values).astype(jnp.bfloat16)
    row_delta = jnp.sum(grad_probs * probs, axis=-1, keepdims=True)
    grad_scores = (probs * (grad_probs - row_delta)).astype(jnp.bfloat16)
    feed_terms = (
        up_weight_term,
        down_weight_term,
        up_bias_term,
        down_bias_term,
        second_gain_term,
        second_shift_term,
    )
    grad_scores, feed_sums = lax.optimization_barrier((grad_scores, feed_reduce(feed_terms)))
    score_scale = 1.0 / math.sqrt(HEAD_DIM)
    grad_queries = jnp.einsum(
        "shqk,skhd->sqhd", grad_scores, key_heads, preferred_element_type=jnp.float32
    )
    grad_queries = (merge_heads(grad_queries) * score_scale).astype(jnp.bfloat16)
    grad_keys = jnp.einsum(
        "shqk,sqhd->skhd", grad_scores, query_heads, preferred_element_type=jnp.float32
    )
    grad_keys = (merge_heads(grad_keys) * score_scale).astype(jnp.bfloat16)
    query_weight_term = times_across(tokens_micro, grad_queries)
    key_weight_term = times_across(tokens_micro, grad_keys)
    value_weight_term = times_across(tokens_micro, grad_values)
    input_grad = (
        grad_first
        + times_back(grad_queries, query_weight)
        + times_back(grad_keys, key_weight)
        + times_back(grad_values, value_weight)
    ).astype(jnp.bfloat16)
    attention_terms = (
        query_weight_term,
        key_weight_term,
        value_weight_term,
        out_weight_term,
        column_sum(grad_queries),
        column_sum(grad_values),
        out_bias_term,
        first_gain_term,
        first_shift_term,
    )
    return (input_grad, attention_terms, feed_sums)


def axis_sizes(device_count):
    side = 1
    while 2 * (2 * side) ** 3 <= device_count:
        side *= 2
    return (device_count // (2 * side * side), side, side, 2)


def axis_digit(sizes, axis):
    stride = math.prod(sizes[axis + 1 :])
    return stride, (lax.axis_index("fsdp") // stride) % sizes[axis]


def shifted_pairs(sizes, axis, shift):
    stride = math.prod(sizes[axis + 1 :])
    pairs = []
    for index in range(math.prod(sizes)):
        digit = (index // stride) % sizes[axis]
        pairs.append((index, index + ((digit + shift) % sizes[axis] - digit) * stride))
    return pairs


def scatter_sum(blocks, sizes, order):
    remaining = [0, 1, 2, 3]
    held = blocks.reshape(sizes + blocks.shape[1:])
    for axis in order:
        place = remaining.index(axis)
        _, digit = axis_digit(sizes, axis)
        held = held.astype(jnp.bfloat16)
        arrived = []
        for shift in range(1, sizes[axis]):
            target = (digit + shift) % sizes[axis]
            part = lax.dynamic_index_in_dim(held, target, place, keepdims=False)
            arrived.append(lax.ppermute(part, "fsdp", shifted_pairs(sizes, axis, shift)))
        own = lax.dynamic_index_in_dim(held, digit, place, keepdims=False)
        held = own.astype(jnp.float32)
        for part in arrived:
            held = held + part.astype(jnp.float32)
        remaining.remove(axis)
    return held


def gather_blocks(own, sizes, order):
    present = []
    held = own
    for axis in order:
        place = sum(1 for other in present if other < axis)
        _, digit = axis_digit(sizes, axis)
        shape = held.shape[:place] + (sizes[axis],) + held.shape[place:]
        joined = lax.dynamic_update_index_in_dim(
            jnp.zeros(shape, held.dtype), held, digit, place
        )
        for shift in range(1, sizes[axis]):
            part = lax.ppermute(held, "fsdp", shifted_pairs(sizes, axis, shift))
            source = (digit - shift) % sizes[axis]
            joined = lax.dynamic_update_index_in_dim(joined, part, source, place)
        held = joined
        present.append(axis)
    return held.reshape((math.prod(sizes),) + own.shape)


X_FIRST = (3, 2, 1, 0)
Y_FIRST = (3, 1, 2, 0)


def pack_rows(pieces, vectors, width, dtype):
    blocks = pieces[0].shape[0]
    line = jnp.concatenate([vector.astype(dtype) for vector in vectors], axis=1)
    used = sum(piece.shape[1] for piece in pieces)
    line_rows = -(-line.shape[1] // width)
    line_rows += -(used + line_rows) % 16
    line = jnp.pad(line, ((0, 0), (0, line_rows * width - line.shape[1])))
    line = line.reshape(blocks, line_rows, width)
    return jnp.concatenate([piece.astype(dtype) for piece in pieces] + [line], axis=1)


def cut_line(line, lengths_of):
    parts = []
    start = 0
    for length in lengths_of:
        parts.append(line[:, start : start + length])
        start += length
    return parts


def shards(
    tokens,
    lengths,
    query_weight,
    key_weight,
    value_weight,
    out_weight,
    query_bias,
    value_bias,
    out_bias,
    first_gain,
    first_shift,
    up_weight,
    down_weight,
    up_bias,
    down_bias,
    second_gain,
    second_shift,
    cotangent,
):
    own_rows, width = query_weight.shape
    feed_rows = down_weight.shape[0]
    fold = up_weight.shape[1] // width
    device_count = width // own_rows
    feed_width = feed_rows * device_count

    def up_pieces(matrix, blocks):
        return [
            matrix[:, part * width : (part + 1) * width].reshape(blocks, -1, width)
            for part in range(fold)
        ]

    sizes = axis_sizes(device_count)

    feed_vectors = (up_bias, down_bias, second_gain, second_shift)
    feed_packed = pack_rows(
        up_pieces(up_weight, 1) + [down_weight[None]],
        [vector[None] for vector in feed_vectors],
        width,
        jnp.bfloat16,
    )
    gathered = lax.all_gather(feed_packed[0], "fsdp", axis=0, tiled=False)
    up_full = jnp.concatenate(
        [
            gathered[:, part * own_rows : (part + 1) * own_rows].reshape(width, width)
            for part in range(fold)
        ],
        axis=1,
    )
    down_start = fold * own_rows
    down_full = gathered[:, down_start : down_start + feed_rows].reshape(feed_width, width)
    line = gathered[:, down_start + feed_rows :].reshape(device_count, -1)
    lines = cut_line(line, [vector.shape[0] for vector in feed_vectors])
    feed_full = (up_full, down_full) + tuple(part.reshape(-1) for part in lines)

    vectors = (query_bias, value_bias, out_bias, first_gain, first_shift)
    near = pack_rows(
        [query_weight[None], key_weight[None]],
        [vector[None] for vector in vectors],
        width,
        jnp.bfloat16,
    )
    near = gather_blocks(near[0], sizes, X_FIRST[::-1])
    far = gather_blocks(
        jnp.concatenate([value_weight, out_weight], axis=0), sizes, Y_FIRST[::-1]
    )
    square = [
        array[:, part * own_rows : (part + 1) * own_rows].reshape(width, width)
        for array in (near, far)
        for part in range(2)
    ]
    line = near[:, 2 * own_rows :].reshape(device_count, -1)
    lines = cut_line(line, [own_rows] * 5)
    attention_full = tuple(square) + tuple(part.reshape(-1) for part in lines)

    output, stored = forward_pass(tokens, lengths, attention_full, feed_full)
    def to_blocks(matrix):
        return matrix.reshape(device_count, -1, width)

    def to_lines(vector):
        return vector.reshape(device_count, -1)

    def feed_reduce(feed_terms):
        up_term, down_term, up_bias_term, down_bias_term, gain_term, shift_term = feed_terms
        down_packed = pack_rows(
            [to_blocks(down_term)],
            [to_lines(part) for part in (up_bias_term, down_bias_term, gain_term, shift_term)],
            width,
            jnp.bfloat16,
        )
        down_sum = scatter_sum(down_packed, sizes, X_FIRST)
        up_sum = scatter_sum(
            jnp.concatenate(
                [part.astype(jnp.bfloat16) for part in up_pieces(up_term, device_count)], axis=1
            ),
            sizes,
            Y_FIRST,
        )
        return (down_sum, up_sum)

    input_grad, attention_terms, (down_sum, up_sum) = backward_pass(
        stored, cotangent, attention_full, feed_full, feed_reduce
    )
    query_term, key_term, value_term, out_term = [to_blocks(part) for part in attention_terms[:4]]
    far_sum = scatter_sum(
        jnp.concatenate([value_term, out_term], axis=1).astype(jnp.bfloat16), sizes, X_FIRST
    )
    near_sum = scatter_sum(
        pack_rows(
            [query_term, key_term],
            [to_lines(part) for part in attention_terms[4:]],
            width,
            jnp.bfloat16,
        ),
        sizes,
        Y_FIRST,
    )
    up_owned = jnp.concatenate(
        [up_sum[part * own_rows : (part + 1) * own_rows] for part in range(fold)], axis=1
    )
    down_owned = down_sum[:feed_rows]
    feed_line = down_sum[feed_rows:].reshape(1, -1)
    feed_vectors = [
        part[0] for part in cut_line(feed_line, [feed_rows, own_rows, own_rows, own_rows])
    ]
    squares_owned = [
        array[part * own_rows : (part + 1) * own_rows]
        for array in (near_sum, far_sum)
        for part in range(2)
    ]
    attention_line = near_sum[2 * own_rows :].reshape(1, -1)
    attention_vectors = [part[0] for part in cut_line(attention_line, [own_rows] * 5)]
    return (
        output,
        input_grad,
        *squares_owned,
        *attention_vectors,
        up_owned,
        down_owned,
        *feed_vectors,
    )


def solution(mesh):
    return jax.shard_map(
        shards,
        mesh=mesh,
        in_specs=(
            P("fsdp", None),
            P("fsdp"),
            P("fsdp", None),
            P("fsdp", None),
            P("fsdp", None),
            P("fsdp", None),
            P("fsdp"),
            P("fsdp"),
            P("fsdp"),
            P("fsdp"),
            P("fsdp"),
            P("fsdp", None),
            P("fsdp", None),
            P("fsdp"),
            P("fsdp"),
            P("fsdp"),
            P("fsdp"),
            P("fsdp", None),
        ),
        out_specs=(
            P("fsdp", None),
            P("fsdp", None),
            P("fsdp", None),
            P("fsdp", None),
            P("fsdp", None),
            P("fsdp", None),
            P("fsdp"),
            P("fsdp"),
            P("fsdp"),
            P("fsdp"),
            P("fsdp"),
            P("fsdp", None),
            P("fsdp", None),
            P("fsdp"),
            P("fsdp"),
            P("fsdp"),
            P("fsdp"),
        ),
        check_vma=False,
    )
```
